256 devices in a mesh: chan: 32 (over z_lo, y, x), inp: 8 (over z_hi, core).
Axes of the slice: x: 4, y: 4, z: 8 (z_hi: 4, z_lo: 2; z = z_hi * 2 + z_lo), core: 2. Of those that a mesh axis runs over, the one named last changes fastest.
Arguments:
- voltages: bfloat16 [1024, 530432], P(('chan', 'inp')), may hold values from -6 to 6
Outputs:
- visibility: float32 [512, 1024, 1024], P(('chan', 'inp'))
The draws below stay inside these ranges and needn't reach their ends.
All inputs are finite; a program needn't handle non-finite values.
Results may differ from the reference program's by a relative error of at most 0.0057.
Values may be sent and summed in bfloat16 or wider, within the bound.
A program may use at most 64 MiB of HBM per device.

```python
import jax
import jax.numpy as jnp
from jax import lax

INPUTS = 1024
FFT_LEN = 2048
NUM_TAPS = 4
SPECTRA = 256
CHANNELS = 512
CHAN_LOW = 256
SAMPLES = 530432


def steps_of(own_key, dims, pieces, smallest, top_value):
    level, own = 1.0, jax.random.fold_in(own_key, 6)
    for axis_at, shards_of in pieces:
        draws = jnp.exp(jax.random.uniform(jax.random.fold_in(own, axis_at), (shards_of,), jnp.float32, smallest / len(pieces), top_value / len(pieces)))
        level = level * jnp.repeat(draws, dims[axis_at] // shards_of).reshape([-1 if axis == axis_at else 1 for axis in range(len(dims))])
    return level


def gaussian(stream_key, dims, spread, most, cuts=(), kind=jnp.bfloat16):
    result = jax.random.normal(stream_key, dims, jnp.float32) * spread
    if len(cuts) > 0:
        result = steps_of(stream_key, dims, cuts, -0.22, 0.18) * result
    return jnp.clip(result, min=-most, max=most).astype(kind)


def setup_inputs(seed: int = 0) -> dict:
    streams_of = jax.random.split(jax.random.key(seed), 2)
    return {
        "voltages": gaussian(streams_of[0], (INPUTS, SAMPLES), 1.0, 6.0, ((0, 256),)),
    }


def make_window():
    index = jnp.arange(NUM_TAPS * FFT_LEN, dtype=jnp.float32)
    shifted = (index + 0.5) / FFT_LEN - NUM_TAPS / 2.0
    taper = 0.54 - 0.46 * jnp.cos(2.0 * jnp.pi * (index + 0.5) / (NUM_TAPS * FFT_LEN))
    return (jnp.sinc(shifted) * taper).reshape(NUM_TAPS, FFT_LEN)

def make_table():
    points = jnp.arange(FFT_LEN, dtype=jnp.int32)[:, None]
    bins = jnp.arange(CHANNELS, dtype=jnp.int32)[None, :] + CHAN_LOW
    phase = (points * bins % FFT_LEN).astype(jnp.float32) * (2.0 * jnp.pi / FFT_LEN)
    norm = 1.0 / jnp.sqrt(jnp.float32(FFT_LEN))
    return jnp.concatenate([jnp.cos(phase) * norm, -jnp.sin(phase) * norm], axis=1).astype(jnp.bfloat16)

def reference(voltages):
    window = make_window()
    frames = voltages.astype(jnp.float32).reshape(INPUTS, SPECTRA + NUM_TAPS - 1, FFT_LEN)
    filtered = jnp.zeros((INPUTS, SPECTRA, FFT_LEN), jnp.float32)
    for tap in range(NUM_TAPS):
        filtered = filtered + frames[:, tap:tap + SPECTRA, :] * window[tap][None, None, :]
    filtered = filtered.astype(jnp.bfloat16)
    table = make_table()
    spectra = jnp.dot(filtered.reshape(INPUTS * SPECTRA, FFT_LEN), table, preferred_element_type=jnp.float32)
    spectra = spectra.astype(jnp.bfloat16).reshape(INPUTS, SPECTRA, 2, CHANNELS)
    by_channel = jnp.transpose(spectra, (3, 0, 1, 2))
    rows = jnp.arange(INPUTS, dtype=jnp.int32)[:, None]
    cols = jnp.arange(INPUTS, dtype=jnp.int32)[None, :]
    upper = rows <= cols

    def one_channel(block):
        values = block.astype(jnp.float32)
        stacked = values.reshape(INPUTS, 2 * SPECTRA)
        rotated = jnp.stack([values[:, :, 1], -values[:, :, 0]], axis=-1).reshape(INPUTS, 2 * SPECTRA)
        real_part = jnp.einsum('as,bs->ab', stacked, stacked)
        imag_part = jnp.einsum('as,bs->ab', rotated, stacked)
        return jnp.where(upper, real_part, imag_part) * (1.0 / SPECTRA)
    return lax.map(one_channel, by_channel)
```

```python
import jax
import jax.numpy as jnp
from jax import lax
from jax.experimental import pallas as pl
from jax.experimental.pallas import tpu as pltpu
from jax.sharding import PartitionSpec as P

FFT_LEN = 2048
CHAN_DEV = 2
NUM_TAPS = 4
SPECTRA = 256
DEVICES = 256
MESH = pl.DeviceIdType.MESH


def make_window():
    index = jnp.arange(NUM_TAPS * FFT_LEN, dtype=jnp.float32)
    shifted = (index + 0.5) / FFT_LEN - NUM_TAPS / 2.0
    taper = 0.54 - 0.46 * jnp.cos(2.0 * jnp.pi * (index + 0.5) / (NUM_TAPS * FFT_LEN))
    return (jnp.sinc(shifted) * taper).reshape(NUM_TAPS, FFT_LEN)


def make_table(channel_total):
    points = jnp.arange(FFT_LEN, dtype=jnp.int32)[:, None]
    bins = jnp.arange(channel_total, dtype=jnp.int32)[None, :] + FFT_LEN // 8
    phase = (points * bins % FFT_LEN).astype(jnp.float32) * (2.0 * jnp.pi / FFT_LEN)
    norm = 1.0 / jnp.sqrt(jnp.float32(FFT_LEN))
    return jnp.concatenate([jnp.cos(phase) * norm, -jnp.sin(phase) * norm], axis=1).astype(
        jnp.bfloat16
    )


def partner(step):
    chan, inp = lax.axis_index("chan"), lax.axis_index("inp")
    x, y, z, core = chan % 4, chan // 4 % 4, inp // 2 * 2 + chan // 16, inp % 2
    core = (core + step % 2) % 2
    z = (z + step // 2 % 8) % 8
    x = (x + step // 16 % 4) % 4
    y = (y + step // 64) % 4
    return z % 2 * 16 + y * 4 + x, z // 2 * 2 + core


def exchange_kernel(send_ref, recv_ref, own_sem, send_sem, recv_sem):
    me = lax.axis_index("chan") * 8 + lax.axis_index("inp")
    barrier = pltpu.get_barrier_semaphore()

    def greet(step, carry):
        pl.semaphore_signal(barrier, inc=1, device_id=partner(step), device_id_type=MESH)
        return carry

    lax.fori_loop(1, DEVICES, greet, 0)
    own = pltpu.make_async_copy(send_ref.at[me], recv_ref.at[me], own_sem)
    own.start()
    pl.semaphore_wait(barrier, DEVICES - 1)

    def send(step, carry):
        chan, inp = partner(step)
        pltpu.make_async_remote_copy(
            src_ref=send_ref.at[chan * 8 + inp],
            dst_ref=recv_ref.at[me],
            send_sem=send_sem,
            recv_sem=recv_sem,
            device_id=(chan, inp),
            device_id_type=MESH,
        ).start()
        return carry

    lax.fori_loop(1, DEVICES, send, 0)
    own.wait()
    all_but_own = pl.ds(0, DEVICES - 1)
    pltpu.make_async_copy(send_ref.at[all_but_own], recv_ref.at[all_but_own], send_sem).wait()
    pltpu.make_async_copy(send_ref.at[all_but_own], recv_ref.at[all_but_own], recv_sem).wait()


def exchange(blocks):
    return pl.pallas_call(
        exchange_kernel,
        out_shape=jax.ShapeDtypeStruct(blocks.shape, blocks.dtype),
        in_specs=[pl.BlockSpec(memory_space=pltpu.VMEM)],
        out_specs=pl.BlockSpec(memory_space=pltpu.VMEM),
        scratch_shapes=[pltpu.SemaphoreType.DMA] * 3,
        compiler_params=pltpu.CompilerParams(
            collective_id=0, has_side_effects=True, vmem_limit_bytes=16 << 20
        ),
        name="exchange",
    )(blocks)


def pair_products(left_re, left_im, right_re, right_im):
    real_part = jnp.einsum("cas,cbs->cab", left_re, right_re, preferred_element_type=jnp.float32)
    real_part = real_part + jnp.einsum(
        "cas,cbs->cab", left_im, right_im, preferred_element_type=jnp.float32
    )
    imag_part = jnp.einsum("cas,cbs->cab", left_im, right_re, preferred_element_type=jnp.float32)
    imag_part = imag_part - jnp.einsum(
        "cas,cbs->cab", left_re, right_im, preferred_element_type=jnp.float32
    )
    return (real_part, imag_part)


def local(voltages):
    local_inputs = voltages.shape[0]
    channel_total = CHAN_DEV * DEVICES
    all_inputs = local_inputs * DEVICES
    window = make_window()
    frames = voltages.reshape(local_inputs, SPECTRA + NUM_TAPS - 1, FFT_LEN)
    filtered = jnp.zeros((local_inputs, SPECTRA, FFT_LEN), jnp.float32)
    for tap in range(NUM_TAPS):
        filtered = (
            filtered
            + frames[:, tap : tap + SPECTRA, :].astype(jnp.float32) * window[tap][None, None, :]
        )
    filtered = filtered.astype(jnp.bfloat16).reshape(local_inputs * SPECTRA, FFT_LEN)
    table = make_table(channel_total)
    spectra = lax.dot_general(
        table, filtered, (((0,), (1,)), ((), ())), preferred_element_type=jnp.float32
    )
    spectra = spectra.astype(jnp.bfloat16).reshape(2, DEVICES, CHAN_DEV, local_inputs, SPECTRA)
    blocks = jnp.transpose(spectra, (1, 0, 2, 3, 4)).reshape(DEVICES, 16, SPECTRA)
    turned = exchange(blocks).reshape(DEVICES, 2, CHAN_DEV, local_inputs, SPECTRA)
    turned = jnp.transpose(turned, (1, 2, 0, 3, 4)).reshape(2, CHAN_DEV, all_inputs, SPECTRA)
    real_in = turned[0]
    imag_in = turned[1]
    scale = 1.0 / SPECTRA
    real_part, imag_part = pair_products(real_in, imag_in, real_in, imag_in)
    rows = jnp.arange(all_inputs, dtype=jnp.int32)[:, None]
    cols = jnp.arange(all_inputs, dtype=jnp.int32)[None, :]
    return jnp.where((rows <= cols)[None], real_part, imag_part) * scale


def solution(mesh):
    in_specs = (P(("chan", "inp"), None),)
    out_specs = P(("chan", "inp"), None, None)
    return jax.shard_map(local, mesh=mesh, in_specs=in_specs, out_specs=out_specs, check_vma=False)
```

```python
import jax
import jax.numpy as jnp
import numpy as np
from jax import lax
from jax.experimental import pallas as pl
from jax.experimental.pallas import tpu as pltpu
from jax.sharding import PartitionSpec as P

FFT_LEN = 2048
CHANNELS = 512
NUM_TAPS = 4
SPECTRA = 256
FRAMES = SPECTRA + NUM_TAPS - 1
INPUTS = 1024
DEVICES = 256
HALF = SPECTRA // 2
MESH = pl.DeviceIdType.MESH


def make_window():
    index = np.arange(NUM_TAPS * FFT_LEN, dtype=np.float64) + 0.5
    shifted = index / FFT_LEN - NUM_TAPS / 2.0
    taper = 0.54 - 0.46 * np.cos(2.0 * np.pi * index / (NUM_TAPS * FFT_LEN))
    window = (np.sinc(shifted) * taper).astype(np.float32).reshape(NUM_TAPS, 16, 1, 128)
    return np.broadcast_to(window, (NUM_TAPS, 16, 4, 128)).reshape(NUM_TAPS, 64, 128)


def make_table():
    bins = np.arange(CHANNELS, dtype=np.int64)[:, None] + FFT_LEN // 8
    phase = (bins * np.arange(FFT_LEN, dtype=np.int64)[None, :] % FFT_LEN) * (2.0 * np.pi / FFT_LEN)
    both = np.stack([np.cos(phase), -np.sin(phase)]) / np.sqrt(FFT_LEN)
    both = both.reshape(2, 2, 4, 32, 2, FFT_LEN).transpose(2, 4, 0, 1, 3, 5)
    return both.reshape(4, 256, FFT_LEN).astype(np.float32).astype(jnp.bfloat16)


def coordinates():
    chan, inp = lax.axis_index("chan"), lax.axis_index("inp")
    return chan % 4, chan // 4 % 4, inp // 2 * 2 + chan // 16, inp % 2


def device_at(x, y, z, core):
    return z % 2 * 16 + y * 4 + x, z // 2 * 2 + core


def away(dx, dy, dz, dcore):
    x, y, z, core = coordinates()
    return device_at((x + dx) % 4, (y + dy) % 4, (z + dz) % 8, (core + dcore) % 2)


def spectra_kernel(
    volt_hbm, window_ref, table_hbm, out_ref,
    volt, table, filtered, send, recv, unpacked,
    volt_sems, table_sems, send_sem, recv_sems, met_sem,
):
    x, y, z, core = coordinates()
    me = (z % 2) * 128 + y * 32 + x * 8 + z // 2 * 2 + core
    barrier = pltpu.get_barrier_semaphore()

    cuts = ((0, 66), (66, 65), (131, 64), (195, 64))
    volt_copies = [
        pltpu.make_async_copy(volt_hbm.at[pl.ds(at, n)], volt.at[pl.ds(at, n)], volt_sems.at[i])
        for i, (at, n) in enumerate(cuts)
    ]
    table_copies = [
        pltpu.make_async_copy(table_hbm.at[(y + g) % 4], table.at[g], table_sems.at[g])
        for g in range(4)
    ]
    for copy in volt_copies[:2] + table_copies[:1] + volt_copies[2:] + table_copies[1:]:
        copy.start()

    def greet(step, carry):
        for target in (away(step % 4, step // 4, 0, 0), away(0, 0, step // 2, step % 2)):
            pl.semaphore_signal(barrier, inc=1, device_id=target, device_id_type=MESH)
        return carry

    lax.fori_loop(1, 16, greet, 0)

    def filter_half(half):
        for q in range(4):
            rows = slice(q * 16, (q + 1) * 16)
            taps = [window_ref[t, rows, :][None] for t in range(NUM_TAPS)]

            def block(i, carry):
                at = pl.multiple_of(half * HALF + i * 16, 16)
                frames = volt[pl.ds(at, 19), rows, :].astype(jnp.float32)
                total = frames[0:16] * taps[0]
                for t in range(1, NUM_TAPS):
                    total = total + frames[t : t + 16] * taps[t]
                total = jnp.transpose(total, (1, 0, 2)).astype(jnp.bfloat16)
                for r in range(16):
                    n, a = q * 4 + r // 4, r % 4
                    to = pl.multiple_of(half * 512 + a * HALF + i * 16, 16)
                    filtered[pl.ds(to, 16), n * 128 : (n + 1) * 128] = total[r]
                return carry

            lax.fori_loop(0, 8, block, 0)

    def transform(g, half):
        parts = []
        for pair in range(2):
            at = half * 512 + pair * 256
            product = lax.dot_general(
                table[g], filtered[at : at + 256, :], (((1,), (1,)), ((), ())),
                preferred_element_type=jnp.float32,
            )
            parts += [product[:, :128].reshape(4, 64, 128), product[:, 128:].reshape(4, 64, 128)]
        block = jnp.concatenate(parts, axis=0)
        send[g, :, half] = jnp.transpose(block, (1, 0, 2)).astype(jnp.bfloat16)

    def send_group(g, half, recv_sem):
        def one(step, carry):
            target = away(step // 16, g, step % 8, step // 8)
            slot = target[0] // 16 * 32 + target[0] % 4 * 8 + target[1]
            source, landing = send.at[g, slot], recv.at[me]
            if half is not None:
                source, landing = source.at[half], landing.at[half]
            pltpu.make_async_remote_copy(
                src_ref=source, dst_ref=landing, send_sem=send_sem, recv_sem=recv_sem,
                device_id=target, device_id_type=MESH,
            ).start()
            return carry

        lax.fori_loop(1 if g == 0 else 0, 64, one, 0)

    def unpack(g):
        for z_lo in range(2):
            first = z_lo * 128 + (y + 4 - g) % 4 * 32
            for half in range(2):
                got = recv[pl.ds(first, 32), half].astype(jnp.float32) * 0.0625
                unpacked[...] = got.reshape(512, 128)
                for comp in range(4):
                    part = unpacked[pl.ds(comp, 128, stride=4), :]
                    to = pl.ds(pl.multiple_of(first * 4, 128), 128)
                    lanes = comp % 2 * 256 + half * 128
                    out_ref[comp // 2, to, lanes : lanes + 128] = part.astype(jnp.bfloat16)
                    if comp % 2 == 0:
                        out_ref[comp // 2, to, 512 + lanes : 640 + lanes] = (-part).astype(jnp.bfloat16)

    for copy in volt_copies[:2]:
        copy.wait()
    filter_half(0)
    pl.semaphore_wait(barrier, 30)

    def meet(step, carry):
        target = away(0, 0, step // 2, step % 2)
        pl.semaphore_signal(met_sem, inc=1, device_id=target, device_id_type=MESH)
        return carry

    lax.fori_loop(1, 16, meet, 0)
    table_copies[0].wait()
    transform(0, 0)
    pl.semaphore_wait(met_sem, 15)
    send_group(0, 0, recv_sems.at[0])
    for copy in volt_copies[2:]:
        copy.wait()
    filter_half(1)
    transform(0, 1)
    send_group(0, 1, recv_sems.at[1])
    for g in range(1, 4):
        table_copies[g].wait()
        transform(g, 0)
        transform(g, 1)
        send_group(g, None, recv_sems.at[g + 1])
    recv[pl.ds(me, 1)] = send[0, pl.ds(z % 2 * 32 + x * 8 + z // 2 * 2 + core, 1)]

    near = recv.at[pl.ds(0, 63), 0]
    pltpu.make_async_copy(near, near, recv_sems.at[0]).wait()
    pltpu.make_async_copy(near, near, recv_sems.at[1]).wait()
    unpack(0)
    far = recv.at[pl.ds(0, 64)]
    for g in range(1, 4):
        pltpu.make_async_copy(far, far, recv_sems.at[g + 1]).wait()
        unpack(g)
    sent = recv.at[pl.ds(0, 255)]
    pltpu.make_async_copy(sent, sent, send_sem).wait()


def spectra_of(voltages, window, table):
    return pl.pallas_call(
        spectra_kernel,
        out_shape=jax.ShapeDtypeStruct((2, INPUTS, 768), jnp.bfloat16),
        in_specs=[
            pl.BlockSpec(memory_space=pltpu.HBM),
            pl.BlockSpec(memory_space=pltpu.VMEM),
            pl.BlockSpec(memory_space=pltpu.HBM),
        ],
        out_specs=pl.BlockSpec(memory_space=pltpu.VMEM),
        scratch_shapes=[
            pltpu.VMEM((FRAMES, 64, 128), jnp.bfloat16),
            pltpu.VMEM((4, 256, FFT_LEN), jnp.bfloat16),
            pltpu.VMEM((1024, FFT_LEN), jnp.bfloat16),
            pltpu.VMEM((4, 64, 2, 16, 128), jnp.bfloat16),
            pltpu.VMEM((DEVICES, 2, 16, 128), jnp.bfloat16),
            pltpu.VMEM((512, 128), jnp.float32),
            pltpu.SemaphoreType.DMA((4,)),
            pltpu.SemaphoreType.DMA((4,)),
            pltpu.SemaphoreType.DMA,
            pltpu.SemaphoreType.DMA((5,)),
            pltpu.SemaphoreType.REGULAR,
        ],
        compiler_params=pltpu.CompilerParams(
            collective_id=0, has_side_effects=True, vmem_limit_bytes=40 << 20
        ),
        name="spectra_exchange",
    )(voltages, window, table)


def gram_kernel(in_ref, out_ref):
    block = pl.program_id(0) % 4
    dims = (((1,), (1,)), ((), ()))
    for k in range(4):

        @pl.when(block == k)
        def _():
            rows = slice(k * 256, (k + 1) * 256)
            real = lax.dot_general(
                in_ref[0, rows, :512], in_ref[0, k * 256 :, :512], dims,
                preferred_element_type=jnp.float32,
            )
            imag = lax.dot_general(
                in_ref[0, rows, 256:], in_ref[0, : (k + 1) * 256, :512], dims,
                preferred_element_type=jnp.float32,
            )
            if k > 0:
                out_ref[0, :, : k * 256] = imag[:, : k * 256]
            down = lax.broadcasted_iota(jnp.int32, (256, 256), 0)
            across = lax.broadcasted_iota(jnp.int32, (256, 256), 1)
            out_ref[0, :, rows] = jnp.where(down <= across, real[:, :256], imag[:, k * 256 :])
            if k < 3:
                out_ref[0, :, (k + 1) * 256 :] = real[:, 256:]


def gram(spectra):
    return pl.pallas_call(
        gram_kernel,
        grid=(8,),
        out_shape=jax.ShapeDtypeStruct((2, INPUTS, INPUTS), jnp.float32),
        in_specs=[pl.BlockSpec((1, INPUTS, 768), lambda i: (i // 4, 0, 0))],
        out_specs=pl.BlockSpec((1, 256, INPUTS), lambda i: (i // 4, i % 4, 0)),
        compiler_params=pltpu.CompilerParams(vmem_limit_bytes=24 << 20),
        name="gram",
    )(spectra)


def local(voltages):
    tiles = voltages.reshape(4, FRAMES * 16, 128).transpose(1, 0, 2).reshape(FRAMES, 64, 128)
    return gram(spectra_of(tiles, jnp.asarray(make_window()), jnp.asarray(make_table())))


def solution(mesh):
    in_specs = (P(("chan", "inp"), None),)
    out_specs = P(("chan", "inp"), None, None)
    return jax.shard_map(local, mesh=mesh, in_specs=in_specs, out_specs=out_specs, check_vma=False)
```

```python
import jax
import jax.numpy as jnp
import numpy as np
from jax import lax
from jax.experimental import pallas as pl
from jax.experimental.pallas import tpu as pltpu
from jax.sharding import PartitionSpec as P

FFT_LEN = 2048
CHANNELS = 512
NUM_TAPS = 4
SPECTRA = 256
FRAMES = SPECTRA + NUM_TAPS - 1
INPUTS = 1024
DEVICES = 256
HALF = SPECTRA // 2
PITCH = 17
WINDOW_PAD = 96
MESH = pl.DeviceIdType.MESH


def make_window():
    index = np.arange(NUM_TAPS * FFT_LEN, dtype=np.float64) + 0.5
    shifted = index / FFT_LEN - NUM_TAPS / 2.0
    taper = 0.54 - 0.46 * np.cos(2.0 * np.pi * index / (NUM_TAPS * FFT_LEN))
    window = (np.sinc(shifted) * taper).astype(np.float32).reshape(NUM_TAPS, 16, 1, 128)
    window = np.broadcast_to(window, (NUM_TAPS, 16, 4, 128)).reshape(NUM_TAPS, 64, 128)
    return np.concatenate([window, np.zeros((WINDOW_PAD - NUM_TAPS, 64, 128), np.float32)])


def make_table():
    bins = np.arange(CHANNELS, dtype=np.int64)[:, None] + FFT_LEN // 8
    phase = (bins * np.arange(FFT_LEN, dtype=np.int64)[None, :] % FFT_LEN) * (2.0 * np.pi / FFT_LEN)
    both = np.stack([np.cos(phase), -np.sin(phase)]) / np.sqrt(FFT_LEN)
    both = both.reshape(2, 2, 4, 32, 2, FFT_LEN).transpose(2, 4, 0, 1, 3, 5)
    return both.reshape(4, 256, FFT_LEN).astype(np.float32).astype(jnp.bfloat16)


def coordinates():
    chan, inp = lax.axis_index("chan"), lax.axis_index("inp")
    return chan % 4, chan // 4 % 4, inp // 2 * 2 + chan // 16, inp % 2


def device_at(x, y, z, core):
    return z % 2 * 16 + y * 4 + x, z // 2 * 2 + core


def away(dx, dy, dz, dcore):
    x, y, z, core = coordinates()
    return device_at((x + dx) % 4, (y + dy) % 4, (z + dz) % 8, (core + dcore) % 2)


def spectra_kernel(
    volt_hbm, window_hbm, table_hbm, out_ref,
    volt, window, table, filtered, turned, send, recv, unpacked,
    volt_sems, window_sem, table_sems, send_sem, recv_sems, met_sem,
):
    x, y, z, core = coordinates()
    me = (z % 2) * 128 + y * 32 + x * 8 + z // 2 * 2 + core
    barrier = pltpu.get_barrier_semaphore()

    def volt_copy(run):
        at = 0 if run == 0 else run * 32 + 3
        frames = pl.ds(at, 35 if run == 0 else 32)
        return pltpu.make_async_copy(volt_hbm.at[frames], volt.at[frames], volt_sems.at[run])

    window_copy = pltpu.make_async_copy(window_hbm.at[pl.ds(0, NUM_TAPS)], window, window_sem)
    table_copies = [
        pltpu.make_async_copy(table_hbm.at[(y + g) % 4], table.at[g], table_sems.at[g])
        for g in range(4)
    ]
    window_copy.start()
    for run in range(4):
        volt_copy(run).start()
    table_copies[0].start()
    for run in range(4, 8):
        volt_copy(run).start()
    for copy in table_copies[1:]:
        copy.start()

    def greet(step, carry):
        for target in (away(step % 4, step // 4, 0, 0), away(0, 0, step // 2, step % 2)):
            pl.semaphore_signal(barrier, inc=1, device_id=target, device_id_type=MESH)
        return carry

    lax.fori_loop(1, 16, greet, 0)

    def filter_run(run):
        volt_copy(run).wait()

        def block(i, carry):
            at = run * 32 + i * 16
            for q in range(4):
                rows = slice(q * 16, (q + 1) * 16)
                taps = [window[t, rows, :] for t in range(NUM_TAPS)]
                frames = []
                for s in range(16 + NUM_TAPS - 1):
                    frames.append(volt[at + s, rows, :].astype(jnp.float32))
                    if s >= NUM_TAPS - 1:
                        terms = [f * tap for f, tap in zip(frames[-NUM_TAPS:], taps)]
                        first = (s - NUM_TAPS + 1) * PITCH
                        total = (terms[0] + terms[1]) + (terms[2] + terms[3])
                        turned[q, first : first + 16, :] = total
                for r in range(16):
                    n, a = q * 4 + r // 4, r % 4
                    to = run // 4 * 512 + a * HALF + run % 4 * 32
                    to = pl.multiple_of(to + i * 16, 16)
                    column = turned[q, pl.ds(r, 16, stride=PITCH), :]
                    filtered[pl.ds(to, 16), n * 128 : (n + 1) * 128] = column.astype(jnp.bfloat16)
            return carry

        lax.fori_loop(0, 2, block, 0)

    def transform(g, half):
        parts = []
        for pair in range(2):
            at = half * 512 + pair * 256
            product = lax.dot_general(
                table[g], filtered[at : at + 256, :], (((1,), (1,)), ((), ())),
                preferred_element_type=jnp.float32,
            )
            parts += [product[:, :128].reshape(4, 64, 128), product[:, 128:].reshape(4, 64, 128)]
        block = jnp.concatenate(parts, axis=0)
        send[g, :, half] = jnp.transpose(block, (1, 0, 2)).astype(jnp.bfloat16)

    def send_group(g, half, first=0, end=64):
        def one(step, carry):
            target = away(step // 16, g, step % 8, step // 8)
            slot = target[0] // 16 * 32 + target[0] % 4 * 8 + target[1]
            source, landing = send.at[g, slot], recv.at[me]
            if half is not None:
                source, landing = source.at[half], landing.at[half]
            pltpu.make_async_remote_copy(
                src_ref=source, dst_ref=landing, send_sem=send_sem, recv_sem=recv_sems.at[g],
                device_id=target, device_id_type=MESH,
            ).start()
            return carry

        lax.fori_loop(first, end, one, 0)

    def unpack(g):
        for z_lo in range(2):
            first = z_lo * 128 + (y + 4 - g) % 4 * 32
            for half in range(2):
                got = recv[pl.ds(first, 32), half].astype(jnp.float32) * 0.0625
                unpacked[...] = got.reshape(512, 128)
                for comp in range(4):
                    part = unpacked[pl.ds(comp, 128, stride=4), :]
                    to = pl.ds(pl.multiple_of(first * 4, 128), 128)
                    lanes = comp % 2 * 256 + half * 128
                    out_ref[comp // 2, to, lanes : lanes + 128] = part.astype(jnp.bfloat16)

    def meet(step, carry):
        target = away(0, 0, step // 2, step % 2)
        pl.semaphore_signal(met_sem, inc=1, device_id=target, device_id_type=MESH)
        return carry

    window_copy.wait()
    for run in range(4):
        filter_run(run)
    pl.semaphore_wait(barrier, 30)
    lax.fori_loop(1, 16, meet, 0)
    table_copies[0].wait()
    transform(0, 0)
    send_group(0, 0, 1, 16)
    pl.semaphore_wait(met_sem, 15)
    send_group(0, 0, 16)
    table_copies[1].wait()
    transform(1, 0)
    send_group(1, 0)
    for run in range(4, 8):
        filter_run(run)
    transform(0, 1)
    send_group(0, 1, 1)
    transform(1, 1)
    send_group(1, 1)
    for g in range(2, 4):
        table_copies[g].wait()
        transform(g, 0)
        transform(g, 1)
        send_group(g, None)
    recv[pl.ds(me, 1)] = send[0, pl.ds(z % 2 * 32 + x * 8 + z // 2 * 2 + core, 1)]

    for g in range(4):
        got = recv.at[pl.ds(0, 63 if g == 0 else 64)]
        pltpu.make_async_copy(got, got, recv_sems.at[g]).wait()
        unpack(g)
    sent = recv.at[pl.ds(0, 255)]
    pltpu.make_async_copy(sent, sent, send_sem).wait()


def spectra_of(voltages, window, table):
    return pl.pallas_call(
        spectra_kernel,
        out_shape=jax.ShapeDtypeStruct((2, INPUTS, 512), jnp.bfloat16),
        in_specs=[
            pl.BlockSpec(memory_space=pltpu.HBM),
            pl.BlockSpec(memory_space=pltpu.HBM),
            pl.BlockSpec(memory_space=pltpu.HBM),
        ],
        out_specs=pl.BlockSpec(memory_space=pltpu.VMEM),
        scratch_shapes=[
            pltpu.VMEM((FRAMES, 64, 128), jnp.bfloat16),
            pltpu.VMEM((NUM_TAPS, 64, 128), jnp.float32),
            pltpu.VMEM((4, 256, FFT_LEN), jnp.bfloat16),
            pltpu.VMEM((1024, FFT_LEN), jnp.bfloat16),
            pltpu.VMEM((4, 16 * PITCH, 128), jnp.float32),
            pltpu.VMEM((4, 64, 2, 16, 128), jnp.bfloat16),
            pltpu.VMEM((DEVICES, 2, 16, 128), jnp.bfloat16),
            pltpu.VMEM((512, 128), jnp.float32),
            pltpu.SemaphoreType.DMA((8,)),
            pltpu.SemaphoreType.DMA,
            pltpu.SemaphoreType.DMA((4,)),
            pltpu.SemaphoreType.DMA,
            pltpu.SemaphoreType.DMA((4,)),
            pltpu.SemaphoreType.REGULAR,
        ],
        compiler_params=pltpu.CompilerParams(
            collective_id=0, has_side_effects=True, vmem_limit_bytes=50 << 20
        ),
        name="spectra_exchange",
    )(voltages, window, table)


def gram_kernel(in_ref, out_hbm, blocks, sems):
    dims = (((1,), (1,)), ((), ()))
    down = lax.broadcasted_iota(jnp.int32, (256, 256), 0)
    across = lax.broadcasted_iota(jnp.int32, (256, 256), 1)
    copies = []
    for c in range(2):
        for k in range(4):
            rows = slice(k * 256, (k + 1) * 256)
            real = lax.dot_general(
                in_ref[c, rows, :], in_ref[c, k * 256 :, :], dims,
                preferred_element_type=jnp.float32,
            )
            turned = jnp.concatenate([in_ref[c, rows, 256:], -in_ref[c, rows, :256]], axis=1)
            imag = lax.dot_general(
                turned, in_ref[c, : (k + 1) * 256, :], dims, preferred_element_type=jnp.float32
            )
            if k > 0:
                blocks[c, rows, : k * 256] = imag[:, : k * 256]
            blocks[c, rows, rows] = jnp.where(down <= across, real[:, :256], imag[:, k * 256 :])
            if k < 3:
                blocks[c, rows, (k + 1) * 256 :] = real[:, 256:]
            copy = pltpu.make_async_copy(blocks.at[c, rows], out_hbm.at[c, rows], sems.at[c * 4 + k])
            copy.start()
            copies.append(copy)
    for copy in copies:
        copy.wait()


def gram(spectra):
    return pl.pallas_call(
        gram_kernel,
        out_shape=jax.ShapeDtypeStruct((2, INPUTS, INPUTS), jnp.float32),
        in_specs=[pl.BlockSpec(memory_space=pltpu.VMEM)],
        out_specs=pl.BlockSpec(memory_space=pltpu.HBM),
        scratch_shapes=[
            pltpu.VMEM((2, INPUTS, INPUTS), jnp.float32),
            pltpu.SemaphoreType.DMA((8,)),
        ],
        compiler_params=pltpu.CompilerParams(vmem_limit_bytes=40 << 20),
        name="gram",
    )(spectra)


def local(voltages):
    tiles = voltages.reshape(4, FRAMES * 16, 128).transpose(1, 0, 2).reshape(FRAMES, 64, 128)
    return gram(spectra_of(tiles, jnp.asarray(make_window()), jnp.asarray(make_table())))


def solution(mesh):
    in_specs = (P(("chan", "inp"), None),)
    out_specs = P(("chan", "inp"), None, None)
    return jax.shard_map(local, mesh=mesh, in_specs=in_specs, out_specs=out_specs, check_vma=False)
```

```python
import jax
import jax.numpy as jnp
import numpy as np
from jax import lax
from jax.experimental import pallas as pl
from jax.experimental.pallas import tpu as pltpu
from jax.sharding import PartitionSpec as P

FFT_LEN = 2048
CHANNELS = 512
NUM_TAPS = 4
SPECTRA = 256
FRAMES = SPECTRA + NUM_TAPS - 1
INPUTS = 1024
DEVICES = 256
HALF = SPECTRA // 2
PITCH = 17
WINDOW_PAD = 96
MESH = pl.DeviceIdType.MESH


def make_window():
    index = np.arange(NUM_TAPS * FFT_LEN, dtype=np.float64) + 0.5
    shifted = index / FFT_LEN - NUM_TAPS / 2.0
    taper = 0.54 - 0.46 * np.cos(2.0 * np.pi * index / (NUM_TAPS * FFT_LEN))
    window = (np.sinc(shifted) * taper).astype(np.float32).reshape(NUM_TAPS, 16, 1, 128)
    window = np.broadcast_to(window, (NUM_TAPS, 16, 4, 128)).reshape(NUM_TAPS, 64, 128)
    return np.concatenate([window, np.zeros((WINDOW_PAD - NUM_TAPS, 64, 128), np.float32)])


def make_table():
    bins = np.arange(CHANNELS, dtype=np.int64)[:, None] + FFT_LEN // 8
    phase = (bins * np.arange(FFT_LEN, dtype=np.int64)[None, :] % FFT_LEN) * (2.0 * np.pi / FFT_LEN)
    both = np.stack([np.cos(phase), -np.sin(phase)]) / np.sqrt(FFT_LEN)
    both = both.reshape(2, 2, 4, 32, 2, FFT_LEN).transpose(2, 4, 0, 1, 3, 5)
    return both.reshape(4, 256, FFT_LEN).astype(np.float32).astype(jnp.bfloat16)


class Torus:
    def __init__(self):
        chan, inp = lax.axis_index("chan"), lax.axis_index("inp")
        self.x, self.y = lax.rem(chan, 4), lax.rem(lax.div(chan, 4), 4)
        self.z, self.core = lax.div(inp, 2) * 2 + lax.div(chan, 16), lax.rem(inp, 2)
        self.flat = chan * 8 + inp
        self.slot = lax.div(chan, 16) * 32 + self.x * 8 + inp
        zs = [lax.rem(self.z + dz, 8) for dz in range(8)]
        self.z_chan = [lax.rem(z, 2) * 16 for z in zs]
        self.z_inp = [lax.div(z, 2) * 2 for z in zs]
        self.lead = [jnp.where(z == 0, 3, jnp.where(z < 3, 2, jnp.where(z == 3, 1, 0))) for z in zs]
        self.y_chan = [lax.rem(self.y + dy, 4) * 4 for dy in range(4)]

    def away(self, dx, dy, dz, dcore):
        x, core = lax.rem(self.x + dx, 4), lax.rem(self.core + dcore, 2)
        inp = self.z_inp[dz] + core
        return (self.z_chan[dz] + self.y_chan[dy] + x, inp), self.z_chan[dz] * 2 + x * 8 + inp


def spectra_kernel(
    volt_hbm, window_hbm, table_hbm, out_ref,
    volt, window, table, filtered, turned, send, recv, unpacked,
    volt_sems, window_sem, table_sems, send_sem, recv_sems, met_sem,
):
    here = Torus()
    me, y = here.flat, here.y
    across = [here.away(0, dy, 0, 0)[0] for dy in range(1, 4)]
    barrier = pltpu.get_barrier_semaphore()

    def volt_copy(run):
        at = 0 if run == 0 else run * 32 + 3
        frames = pl.ds(at, 35 if run == 0 else 32)
        return pltpu.make_async_copy(volt_hbm.at[frames], volt.at[frames], volt_sems.at[run])

    window_copy = pltpu.make_async_copy(window_hbm.at[pl.ds(0, NUM_TAPS)], window, window_sem)
    table_copies = [
        pltpu.make_async_copy(table_hbm.at[lax.rem(y + g, 4)], table.at[g], table_sems.at[g])
        for g in range(4)
    ]
    window_copy.start()
    volt_copy(0).start()
    volt_copy(1).start()

    def greet(dx, dcore, first=0):
        for dz in range(first, 8):
            target = here.away(dx, 0, dz, dcore)[0]
            pl.semaphore_signal(barrier, inc=1, device_id=target, device_id_type=MESH)

    def greet_eight(k, carry):
        greet(lax.div(k, 2), lax.rem(k, 2))
        return carry

    greet(0, 0, 1)
    lax.fori_loop(1, 8, greet_eight, 0)
    for target in across:
        pl.semaphore_signal(barrier, inc=1, device_id=target, device_id_type=MESH)
    volt_copy(2).start()
    volt_copy(3).start()
    table_copies[0].start()
    for run in range(4, 8):
        volt_copy(run).start()
    for copy in table_copies[1:]:
        copy.start()

    def filter_run(run):
        volt_copy(run).wait()

        def block(i, carry):
            at = run * 32 + i * 16
            for q in range(4):
                rows = slice(q * 16, (q + 1) * 16)
                taps = [window[t, rows, :] for t in range(NUM_TAPS)]
                frames = []
                for s in range(16 + NUM_TAPS - 1):
                    frames.append(volt[at + s, rows, :].astype(jnp.float32))
                    if s >= NUM_TAPS - 1:
                        terms = [f * tap for f, tap in zip(frames[-NUM_TAPS:], taps)]
                        first = (s - NUM_TAPS + 1) * PITCH
                        total = (terms[0] + terms[1]) + (terms[2] + terms[3])
                        turned[q, first : first + 16, :] = total
                for r in range(16):
                    n, a = q * 4 + r // 4, r % 4
                    to = run // 4 * 512 + a * HALF + run % 4 * 32
                    to = pl.multiple_of(to + i * 16, 16)
                    column = turned[q, pl.ds(r, 16, stride=PITCH), :]
                    filtered[pl.ds(to, 16), n * 128 : (n + 1) * 128] = column.astype(jnp.bfloat16)
            return carry

        lax.fori_loop(0, 2, block, 0)

    def transform(g, half):
        parts = []
        for pair in range(2):
            at = half * 512 + pair * 256
            product = lax.dot_general(
                table[g], filtered[at : at + 256, :], (((1,), (1,)), ((), ())),
                preferred_element_type=jnp.float32,
            )
            parts += [product[:, :128].reshape(4, 64, 128), product[:, 128:].reshape(4, 64, 128)]
        block = jnp.concatenate(parts, axis=0)
        send[g, :, half] = jnp.transpose(block, (1, 0, 2)).astype(jnp.bfloat16)

    def send_eight(g, half, dx, dcore, first=0):
        for dz in range(first, 8):
            target, slot = here.away(dx, g, dz, dcore)
            source, landing = send.at[g, slot], recv.at[me]
            if half is not None:
                source, landing = source.at[half], landing.at[half]
            pltpu.make_async_remote_copy(
                src_ref=source, dst_ref=landing, send_sem=send_sem, recv_sem=recv_sems.at[g],
                device_id=target, device_id_type=MESH,
            ).start()

    def send_group(g, half, first=0):
        def eight(k, carry):
            send_eight(g, half, lax.div(k, 2), lax.rem(k, 2))
            return carry

        lax.fori_loop(first, 8, eight, 0)

    def unpack(g):
        for z_lo in range(2):
            first = z_lo * 128 + lax.rem(y + 4 - g, 4) * 32
            for half in range(2):
                got = recv[pl.ds(first, 32), half].astype(jnp.float32) * 0.0625
                unpacked[...] = got.reshape(512, 128)
                for comp in range(4):
                    part = unpacked[pl.ds(comp, 128, stride=4), :]
                    to = pl.ds(pl.multiple_of(first * 4, 128), 128)
                    lanes = comp % 2 * 256 + half * 128
                    out_ref[comp // 2, to, lanes : lanes + 128] = part.astype(jnp.bfloat16)

    window_copy.wait()
    for run in range(4):
        filter_run(run)
    pl.semaphore_wait(barrier, 66)
    for target in across:
        pl.semaphore_signal(met_sem, inc=1, device_id=target, device_id_type=MESH)
    table_copies[0].wait()
    transform(0, 0)
    send_eight(0, 0, 0, 0, 1)
    send_group(0, 0, 1)
    pl.semaphore_wait(met_sem, 3)
    table_copies[1].wait()
    transform(1, 0)
    send_group(1, 0)
    for run in range(4, 8):
        filter_run(run)
    transform(0, 1)
    send_eight(0, 1, 0, 0, 1)
    send_group(0, 1, 1)
    transform(1, 1)
    send_group(1, 1)
    for g in range(2, 4):
        table_copies[g].wait()
        transform(g, 0)
        transform(g, 1)

    def send_one(j, dz):
        g, k = lax.div(j, 8), lax.rem(j, 8)
        x, core = lax.rem(here.x + lax.div(k, 2), 4), lax.rem(here.core + lax.rem(k, 2), 2)
        inp = here.z_inp[dz] + core
        target = (here.z_chan[dz] + lax.rem(here.y + 2 + g, 4) * 4 + x, inp)
        pltpu.make_async_remote_copy(
            src_ref=send.at[2 + g, here.z_chan[dz] * 2 + x * 8 + inp], dst_ref=recv.at[me],
            send_sem=send_sem, recv_sem=recv_sems.at[2 + g],
            device_id=target, device_id_type=MESH,
        ).start()

    def rounds(j, carry):
        for dz in range(8):
            lead = here.lead[dz]

            @pl.when(j < 16 - lead)
            def _():
                send_one(j, dz)

            @pl.when((lax.rem(j, 4) == 3) & (lax.div(j, 4) < lead))
            def _():
                send_one(16 - lead + lax.div(j, 4), dz)

        return carry

    lax.fori_loop(0, 16, rounds, 0)
    recv[pl.ds(me, 1)] = send[0, pl.ds(here.slot, 1)]

    for g in range(4):
        got = recv.at[pl.ds(0, 63 if g == 0 else 64)]
        pltpu.make_async_copy(got, got, recv_sems.at[g]).wait()
        unpack(g)
    sent = recv.at[pl.ds(0, 255)]
    pltpu.make_async_copy(sent, sent, send_sem).wait()


def spectra_of(voltages, window, table):
    return pl.pallas_call(
        spectra_kernel,
        out_shape=jax.ShapeDtypeStruct((2, INPUTS, 512), jnp.bfloat16),
        in_specs=[
            pl.BlockSpec(memory_space=pltpu.HBM),
            pl.BlockSpec(memory_space=pltpu.HBM),
            pl.BlockSpec(memory_space=pltpu.HBM),
        ],
        out_specs=pl.BlockSpec(memory_space=pltpu.VMEM),
        scratch_shapes=[
            pltpu.VMEM((FRAMES, 64, 128), jnp.bfloat16),
            pltpu.VMEM((NUM_TAPS, 64, 128), jnp.float32),
            pltpu.VMEM((4, 256, FFT_LEN), jnp.bfloat16),
            pltpu.VMEM((1024, FFT_LEN), jnp.bfloat16),
            pltpu.VMEM((4, 16 * PITCH, 128), jnp.float32),
            pltpu.VMEM((4, 64, 2, 16, 128), jnp.bfloat16),
            pltpu.VMEM((DEVICES, 2, 16, 128), jnp.bfloat16),
            pltpu.VMEM((512, 128), jnp.float32),
            pltpu.SemaphoreType.DMA((8,)),
            pltpu.SemaphoreType.DMA,
            pltpu.SemaphoreType.DMA((4,)),
            pltpu.SemaphoreType.DMA,
            pltpu.SemaphoreType.DMA((4,)),
            pltpu.SemaphoreType.REGULAR,
        ],
        compiler_params=pltpu.CompilerParams(
            collective_id=0, has_side_effects=True, vmem_limit_bytes=50 << 20
        ),
        name="spectra_exchange",
    )(voltages, window, table)


def gram_kernel(in_ref, out_hbm, blocks, sems):
    dims = (((1,), (1,)), ((), ()))
    down = lax.broadcasted_iota(jnp.int32, (256, 256), 0)
    across = lax.broadcasted_iota(jnp.int32, (256, 256), 1)
    copies = []
    for c in range(2):
        for k in range(4):
            rows = slice(k * 256, (k + 1) * 256)
            real = lax.dot_general(
                in_ref[c, rows, :], in_ref[c, k * 256 :, :], dims,
                preferred_element_type=jnp.float32,
            )
            turned = jnp.concatenate([in_ref[c, rows, 256:], -in_ref[c, rows, :256]], axis=1)
            imag = lax.dot_general(
                turned, in_ref[c, : (k + 1) * 256, :], dims, preferred_element_type=jnp.float32
            )
            if k > 0:
                blocks[c, rows, : k * 256] = imag[:, : k * 256]
            blocks[c, rows, rows] = jnp.where(down <= across, real[:, :256], imag[:, k * 256 :])
            if k < 3:
                blocks[c, rows, (k + 1) * 256 :] = real[:, 256:]
            copy = pltpu.make_async_copy(blocks.at[c, rows], out_hbm.at[c, rows], sems.at[c * 4 + k])
            copy.start()
            copies.append(copy)
    for copy in copies:
        copy.wait()


def gram(spectra):
    return pl.pallas_call(
        gram_kernel,
        out_shape=jax.ShapeDtypeStruct((2, INPUTS, INPUTS), jnp.float32),
        in_specs=[pl.BlockSpec(memory_space=pltpu.VMEM)],
        out_specs=pl.BlockSpec(memory_space=pltpu.HBM),
        scratch_shapes=[
            pltpu.VMEM((2, INPUTS, INPUTS), jnp.float32),
            pltpu.SemaphoreType.DMA((8,)),
        ],
        compiler_params=pltpu.CompilerParams(vmem_limit_bytes=40 << 20),
        name="gram",
    )(spectra)


def local(voltages):
    tiles = voltages.reshape(4, FRAMES * 16, 128).transpose(1, 0, 2).reshape(FRAMES, 64, 128)
    return gram(spectra_of(tiles, jnp.asarray(make_window()), jnp.asarray(make_table())))


def solution(mesh):
    in_specs = (P(("chan", "inp"), None),)
    out_specs = P(("chan", "inp"), None, None)
    return jax.shard_map(local, mesh=mesh, in_specs=in_specs, out_specs=out_specs, check_vma=False)
```

```python
import jax
import jax.numpy as jnp
import numpy as np
from jax import lax
from jax.experimental import pallas as pl
from jax.experimental.pallas import tpu as pltpu
from jax.sharding import PartitionSpec as P

FFT_LEN = 2048
CHANNELS = 512
NUM_TAPS = 4
SPECTRA = 256
FRAMES = SPECTRA + NUM_TAPS - 1
INPUTS = 1024
DEVICES = 256
HALF = SPECTRA // 2
PITCH = 17
WINDOW_PAD = 192
MESH = pl.DeviceIdType.MESH


def make_window():
    index = np.arange(NUM_TAPS * FFT_LEN, dtype=np.float64) + 0.5
    shifted = index / FFT_LEN - NUM_TAPS / 2.0
    taper = 0.54 - 0.46 * np.cos(2.0 * np.pi * index / (NUM_TAPS * FFT_LEN))
    window = (np.sinc(shifted) * taper).astype(np.float32).reshape(NUM_TAPS, 16, 1, 128)
    window = np.broadcast_to(window, (NUM_TAPS, 16, 4, 128)).reshape(NUM_TAPS, 64, 128)
    return np.concatenate([window, np.zeros((WINDOW_PAD - NUM_TAPS, 64, 128), np.float32)])


def make_table():
    bins = np.arange(CHANNELS, dtype=np.int64)[:, None] + FFT_LEN // 8
    phase = (bins * np.arange(FFT_LEN, dtype=np.int64)[None, :] % FFT_LEN) * (2.0 * np.pi / FFT_LEN)
    both = np.stack([np.cos(phase), -np.sin(phase)]) / np.sqrt(FFT_LEN)
    both = both.reshape(2, 2, 4, 32, 2, FFT_LEN).transpose(2, 4, 0, 1, 3, 5)
    return both.reshape(4, 256, FFT_LEN).astype(np.float32).astype(jnp.bfloat16)


class Torus:
    def __init__(self):
        chan, inp = lax.axis_index("chan"), lax.axis_index("inp")
        self.x, self.y = lax.rem(chan, 4), lax.rem(lax.div(chan, 4), 4)
        self.z, self.core = lax.div(inp, 2) * 2 + lax.div(chan, 16), lax.rem(inp, 2)
        self.flat = chan * 8 + inp
        self.slot = lax.div(chan, 16) * 32 + self.x * 8 + inp
        zs = [lax.rem(self.z + dz, 8) for dz in range(8)]
        self.z_chan = [lax.rem(z, 2) * 16 for z in zs]
        self.z_inp = [lax.div(z, 2) * 2 for z in zs]
        self.lead = [jnp.where(z == 0, 6, jnp.where(z < 3, 4, jnp.where(z == 3, 2, 0))) for z in zs]
        self.y_chan = [lax.rem(self.y + dy, 4) * 4 for dy in range(4)]

    def away(self, dx, dy, dz, dcore):
        x, core = lax.rem(self.x + dx, 4), lax.rem(self.core + dcore, 2)
        inp = self.z_inp[dz] + core
        return (self.z_chan[dz] + self.y_chan[dy] + x, inp), self.z_chan[dz] * 2 + x * 8 + inp

    def across(self, dx, dy):
        x = self.x + (1 - 2 * lax.rem(self.x, 2)) * dx
        return self.z_chan[0] + self.y_chan[dy] + x, self.z_inp[0] + self.core


def gram_rows(in_ref, out_ref, k):
    dims = (((1,), (1,)), ((), ()))
    rows = slice(k * 256, (k + 1) * 256)
    real = lax.dot_general(
        in_ref[rows, :], in_ref[k * 256 :, :], dims, preferred_element_type=jnp.float32
    )
    turned = jnp.concatenate([in_ref[rows, 256:], -in_ref[rows, :256]], axis=1)
    imag = lax.dot_general(
        turned, in_ref[: (k + 1) * 256, :], dims, preferred_element_type=jnp.float32
    )
    down = lax.broadcasted_iota(jnp.int32, (256, 256), 0)
    across = lax.broadcasted_iota(jnp.int32, (256, 256), 1)
    if k > 0:
        out_ref[rows, : k * 256] = imag[:, : k * 256]
    out_ref[rows, rows] = jnp.where(down <= across, real[:, :256], imag[:, k * 256 :])
    if k < 3:
        out_ref[rows, (k + 1) * 256 :] = real[:, 256:]


def spectra_kernel(
    volt_hbm, window_hbm, table_hbm, first_ref, second_ref,
    volt, window, table, filtered, turned, send, recv, unpacked, channel,
    volt_sems, window_sem, table_sems, send_sem, recv_sems, met_sem,
):
    here = Torus()
    me, y = here.flat, here.y
    across = [here.across(dx, dy) for dx in range(2) for dy in range(4) if dx + dy > 0]
    barrier = pltpu.get_barrier_semaphore()

    def volt_copy(run):
        at = 0 if run == 0 else run * 32 + 3
        frames = pl.ds(at, 35 if run == 0 else 32)
        return pltpu.make_async_copy(volt_hbm.at[frames], volt.at[frames], volt_sems.at[run])

    window_copy = pltpu.make_async_copy(window_hbm.at[pl.ds(0, NUM_TAPS)], window, window_sem)
    table_copies = [
        pltpu.make_async_copy(table_hbm.at[lax.rem(y + g, 4)], table.at[g], table_sems.at[g])
        for g in range(4)
    ]
    window_copy.start()
    volt_copy(0).start()
    volt_copy(1).start()

    def greet(dx, dcore, first=0):
        for dz in range(first, 8):
            target = here.away(dx, 0, dz, dcore)[0]
            pl.semaphore_signal(barrier, inc=1, device_id=target, device_id_type=MESH)

    greet(0, 0, 1)
    greet(0, 1)
    greet(2, 0)
    greet(2, 1)
    for target in across:
        pl.semaphore_signal(barrier, inc=1, device_id=target, device_id_type=MESH)
    volt_copy(2).start()
    volt_copy(3).start()
    table_copies[0].start()
    for run in range(4, 8):
        volt_copy(run).start()
    for copy in table_copies[1:]:
        copy.start()

    def filter_run(run):
        volt_copy(run).wait()

        def block(i, carry):
            at = run * 32 + i * 16
            for q in range(4):
                rows = slice(q * 16, (q + 1) * 16)
                taps = [window[t, rows, :] for t in range(NUM_TAPS)]
                frames = []
                for s in range(16 + NUM_TAPS - 1):
                    frames.append(volt[at + s, rows, :].astype(jnp.float32))
                    if s >= NUM_TAPS - 1:
                        terms = [f * tap for f, tap in zip(frames[-NUM_TAPS:], taps)]
                        first = (s - NUM_TAPS + 1) * PITCH
                        total = (terms[0] + terms[1]) + (terms[2] + terms[3])
                        turned[q, first : first + 16, :] = total
                for r in range(16):
                    n, a = q * 4 + r // 4, r % 4
                    to = run // 4 * 512 + a * HALF + run % 4 * 32
                    to = pl.multiple_of(to + i * 16, 16)
                    column = turned[q, pl.ds(r, 16, stride=PITCH), :]
                    filtered[pl.ds(to, 16), n * 128 : (n + 1) * 128] = column.astype(jnp.bfloat16)
            return carry

        lax.fori_loop(0, 2, block, 0)

    def products(g, half):
        parts = []
        for pair in range(2):
            at = half * 512 + pair * 256
            product = lax.dot_general(
                table[g], filtered[at : at + 256, :], (((1,), (1,)), ((), ())),
                preferred_element_type=jnp.float32,
            )
            parts += [product[:, :128].reshape(4, 64, 128), product[:, 128:].reshape(4, 64, 128)]
        return parts

    def transform(g, half):
        block = jnp.concatenate(products(g, half), axis=0)
        send[g, :, half] = jnp.transpose(block, (1, 0, 2)).astype(jnp.bfloat16)

    def transform_channels(g):
        halves = [products(g, 0), products(g, 1)]
        for c in range(2):
            rows = [halves[h][a][c * 2 : c * 2 + 2] for a in range(4) for h in range(2)]
            block = jnp.concatenate(rows, axis=0)
            send[g, :, c] = jnp.transpose(block, (1, 0, 2)).astype(jnp.bfloat16)

    def send_eight(g, tile, dx, dcore, first=0):
        for dz in range(first, 8):
            target, slot = here.away(dx, g, dz, dcore)
            pltpu.make_async_remote_copy(
                src_ref=send.at[g, slot, tile], dst_ref=recv.at[me, tile],
                send_sem=send_sem, recv_sem=recv_sems.at[g, tile],
                device_id=target, device_id_type=MESH,
            ).start()

    def send_group(g, tile, first=0):
        def eight(k, carry):
            send_eight(g, tile, lax.div(k, 2), lax.rem(k, 2))
            return carry

        lax.fori_loop(first, 8, eight, 0)

    def unpack(g, tile):
        got = recv.at[pl.ds(0, 63 if g == 0 else 64), 0]
        pltpu.make_async_copy(got, got, recv_sems.at[g, tile]).wait()
        for z_lo in range(2):
            first = z_lo * 128 + lax.rem(y + 4 - g, 4) * 32
            values = recv[pl.ds(first, 32), tile].astype(jnp.float32) * 0.0625
            unpacked[...] = values.reshape(512, 128)
            to = pl.ds(pl.multiple_of(first * 4, 128), 128)
            for k in range(4):
                part = unpacked[pl.ds(k, 128, stride=4), :].astype(jnp.bfloat16)
                c, half = (k // 2, tile) if g < 2 else (tile, k // 2)
                lanes = k % 2 * 256 + half * 128
                (channel, second_ref)[c][to, lanes : lanes + 128] = part

    window_copy.wait()
    for run in range(4):
        filter_run(run)
    pl.semaphore_wait(barrier, 38)
    for target in across:
        pl.semaphore_signal(met_sem, inc=1, device_id=target, device_id_type=MESH)
    table_copies[0].wait()
    transform(0, 0)
    send_eight(0, 0, 0, 0, 1)
    send_eight(0, 0, 0, 1)
    send_eight(0, 0, 2, 0)
    send_eight(0, 0, 2, 1)
    pl.semaphore_wait(met_sem, 7)
    for dx in (1, 3):
        send_eight(0, 0, dx, 0)
        send_eight(0, 0, dx, 1)
    table_copies[1].wait()
    transform(1, 0)
    send_group(1, 0)
    for run in range(4, 8):
        filter_run(run)
    transform(0, 1)
    send_eight(0, 1, 0, 0, 1)
    send_group(0, 1, 1)
    transform(1, 1)
    send_group(1, 1)
    for g in range(2, 4):
        table_copies[g].wait()
        transform_channels(g)

    def send_one(j, dz):
        tile, g, k = lax.div(j, 16), lax.rem(lax.div(j, 8), 2), lax.rem(j, 8)
        x, core = lax.rem(here.x + lax.div(k, 2), 4), lax.rem(here.core + lax.rem(k, 2), 2)
        inp = here.z_inp[dz] + core
        target = (here.z_chan[dz] + lax.rem(here.y + 2 + g, 4) * 4 + x, inp)
        pltpu.make_async_remote_copy(
            src_ref=send.at[2 + g, here.z_chan[dz] * 2 + x * 8 + inp, tile], dst_ref=recv.at[me, tile],
            send_sem=send_sem, recv_sem=recv_sems.at[2 + g, tile],
            device_id=target, device_id_type=MESH,
        ).start()

    def to_origin(j, dz):
        k = lax.rem(j, 8)
        apart = lax.rem(here.x + lax.div(k, 2), 4) + lax.rem(here.y + 2 + lax.rem(lax.div(j, 8), 2), 4)
        core = lax.rem(here.core + lax.rem(k, 2), 2)
        return apart + here.z_chan[dz] + here.z_inp[dz] + 1 - core == 0

    def rounds(j, carry):
        for dz in range(8):
            lead = jnp.where(to_origin(j, dz), 16, here.lead[dz])

            @pl.when(j < 32 - lead)
            def _():
                send_one(j, dz)

            ahead = 32 - here.lead[dz] + lax.div(j, 4)

            @pl.when((lax.rem(j, 4) == 3) & (ahead < 32))
            def _():
                @pl.when(jnp.logical_not(to_origin(ahead, dz)))
                def _():
                    send_one(ahead, dz)

            @pl.when((j < 16) & to_origin(j, dz))
            def _():
                send_one(j + 16, dz)

        return carry

    lax.fori_loop(0, 32, rounds, 0)
    recv[pl.ds(me, 1)] = send[0, pl.ds(here.slot, 1)]

    for g, tile in ((0, 0), (1, 0), (0, 1), (1, 1), (2, 0), (3, 0)):
        unpack(g, tile)
    for k in range(4):
        gram_rows(channel, first_ref, k)
    unpack(2, 1)
    unpack(3, 1)
    sent = recv.at[pl.ds(0, 255)]
    pltpu.make_async_copy(sent, sent, send_sem).wait()


def spectra_of(voltages, window, table):
    return pl.pallas_call(
        spectra_kernel,
        out_shape=(
            jax.ShapeDtypeStruct((INPUTS, INPUTS), jnp.float32),
            jax.ShapeDtypeStruct((INPUTS, 512), jnp.bfloat16),
        ),
        in_specs=[
            pl.BlockSpec(memory_space=pltpu.HBM),
            pl.BlockSpec(memory_space=pltpu.HBM),
            pl.BlockSpec(memory_space=pltpu.HBM),
        ],
        out_specs=(pl.BlockSpec(memory_space=pltpu.VMEM),) * 2,
        scratch_shapes=[
            pltpu.VMEM((FRAMES, 64, 128), jnp.bfloat16),
            pltpu.VMEM((NUM_TAPS, 64, 128), jnp.float32),
            pltpu.VMEM((4, 256, FFT_LEN), jnp.bfloat16),
            pltpu.VMEM((1024, FFT_LEN), jnp.bfloat16),
            pltpu.VMEM((4, 16 * PITCH, 128), jnp.float32),
            pltpu.VMEM((4, 64, 2, 16, 128), jnp.bfloat16),
            pltpu.VMEM((DEVICES, 2, 16, 128), jnp.bfloat16),
            pltpu.VMEM((512, 128), jnp.float32),
            pltpu.VMEM((INPUTS, 512), jnp.bfloat16),
            pltpu.SemaphoreType.DMA((8,)),
            pltpu.SemaphoreType.DMA,
            pltpu.SemaphoreType.DMA((4,)),
            pltpu.SemaphoreType.DMA,
            pltpu.SemaphoreType.DMA((4, 2)),
            pltpu.SemaphoreType.REGULAR,
        ],
        compiler_params=pltpu.CompilerParams(
            collective_id=0, has_side_effects=True, vmem_limit_bytes=45 << 20
        ),
        name="spectra_exchange",
    )(voltages, window, table)


def gram_kernel(first_ref, in_ref, out_hbm, blocks, first_sems, sems):
    copies = []
    for k in range(2):
        rows = slice(k * 512, (k + 1) * 512)
        copies.append(pltpu.make_async_copy(first_ref.at[rows], out_hbm.at[0, rows], first_sems.at[k]))
        copies[-1].start()
    for k in range(4):
        rows = slice(k * 256, (k + 1) * 256)
        gram_rows(in_ref, blocks, k)
        copies.append(pltpu.make_async_copy(blocks.at[rows], out_hbm.at[1, rows], sems.at[k]))
        copies[-1].start()
    for copy in copies:
        copy.wait()


def gram(first, spectra):
    return pl.pallas_call(
        gram_kernel,
        out_shape=jax.ShapeDtypeStruct((2, INPUTS, INPUTS), jnp.float32),
        in_specs=[pl.BlockSpec(memory_space=pltpu.VMEM)] * 2,
        out_specs=pl.BlockSpec(memory_space=pltpu.HBM),
        scratch_shapes=[
            pltpu.VMEM((INPUTS, INPUTS), jnp.float32),
            pltpu.SemaphoreType.DMA((2,)),
            pltpu.SemaphoreType.DMA((4,)),
        ],
        compiler_params=pltpu.CompilerParams(vmem_limit_bytes=40 << 20),
        name="gram",
    )(first, spectra)


def local(voltages):
    tiles = voltages.reshape(4, FRAMES * 16, 128).transpose(1, 0, 2).reshape(FRAMES, 64, 128)
    return gram(*spectra_of(tiles, jnp.asarray(make_window()), jnp.asarray(make_table())))


def solution(mesh):
    in_specs = (P(("chan", "inp"), None),)
    out_specs = P(("chan", "inp"), None, None)
    return jax.shard_map(local, mesh=mesh, in_specs=in_specs, out_specs=out_specs, check_vma=False)
```

```python
import jax
import jax.numpy as jnp
import numpy as np
from jax import lax
from jax.experimental import pallas as pl
from jax.experimental.pallas import tpu as pltpu
from jax.sharding import PartitionSpec as P

FFT_LEN = 2048
CHANNELS = 512
NUM_TAPS = 4
SPECTRA = 256
FRAMES = SPECTRA + NUM_TAPS - 1
INPUTS = 1024
DEVICES = 256
HALF = SPECTRA // 2
PITCH = 17
WINDOW_PAD = 192
MESH = pl.DeviceIdType.MESH


def make_window():
    index = np.arange(NUM_TAPS * FFT_LEN, dtype=np.float64) + 0.5
    shifted = index / FFT_LEN - NUM_TAPS / 2.0
    taper = 0.54 - 0.46 * np.cos(2.0 * np.pi * index / (NUM_TAPS * FFT_LEN))
    window = (np.sinc(shifted) * taper).astype(np.float32).reshape(NUM_TAPS, 16, 1, 128)
    window = np.broadcast_to(window, (NUM_TAPS, 16, 4, 128)).reshape(NUM_TAPS, 64, 128)
    return np.concatenate([window, np.zeros((WINDOW_PAD - NUM_TAPS, 64, 128), np.float32)])


def make_table():
    bins = np.arange(CHANNELS, dtype=np.int64)[:, None] + FFT_LEN // 8
    phase = (bins * np.arange(FFT_LEN, dtype=np.int64)[None, :] % FFT_LEN) * (2.0 * np.pi / FFT_LEN)
    both = np.stack([np.cos(phase), -np.sin(phase)]) / np.sqrt(FFT_LEN)
    both = both.reshape(2, 2, 4, 32, 2, FFT_LEN).transpose(2, 4, 0, 1, 3, 5)
    return both.reshape(4, 256, FFT_LEN).astype(np.float32).astype(jnp.bfloat16)


class Torus:
    def __init__(self):
        chan, inp = lax.axis_index("chan"), lax.axis_index("inp")
        self.x, self.y = lax.rem(chan, 4), lax.rem(lax.div(chan, 4), 4)
        self.z, self.core = lax.div(inp, 2) * 2 + lax.div(chan, 16), lax.rem(inp, 2)
        self.flat = chan * 8 + inp
        self.slot = lax.div(chan, 16) * 32 + self.x * 8 + inp
        zs = [lax.rem(self.z + dz, 8) for dz in range(8)]
        self.z_chan = [lax.rem(z, 2) * 16 for z in zs]
        self.z_inp = [lax.div(z, 2) * 2 for z in zs]
        self.lead = [jnp.where(z == 0, 6, jnp.where(z < 3, 4, jnp.where(z == 3, 2, 0))) for z in zs]
        self.y_chan = [lax.rem(self.y + dy, 4) * 4 for dy in range(4)]

    def away(self, dx, dy, dz, dcore):
        x, core = lax.rem(self.x + dx, 4), lax.rem(self.core + dcore, 2)
        inp = self.z_inp[dz] + core
        return (self.z_chan[dz] + self.y_chan[dy] + x, inp), self.z_chan[dz] * 2 + x * 8 + inp

    def across(self, dx, dy):
        x = self.x + (1 - 2 * lax.rem(self.x, 2)) * dx
        return self.z_chan[0] + self.y_chan[dy] + x, self.z_inp[0] + self.core


def gram_rows(in_ref, out_ref, k):
    dims = (((1,), (1,)), ((), ()))
    rows = slice(k * 256, (k + 1) * 256)
    real = lax.dot_general(
        in_ref[rows, :], in_ref[k * 256 :, :], dims, preferred_element_type=jnp.float32
    )
    turned = jnp.concatenate([in_ref[rows, 256:], -in_ref[rows, :256]], axis=1)
    imag = lax.dot_general(
        turned, in_ref[: (k + 1) * 256, :], dims, preferred_element_type=jnp.float32
    )
    down = lax.broadcasted_iota(jnp.int32, (256, 256), 0)
    across = lax.broadcasted_iota(jnp.int32, (256, 256), 1)
    if k > 0:
        out_ref[rows, : k * 256] = imag[:, : k * 256]
    out_ref[rows, rows] = jnp.where(down <= across, real[:, :256], imag[:, k * 256 :])
    if k < 3:
        out_ref[rows, (k + 1) * 256 :] = real[:, 256:]


def spectra_kernel(
    volt_hbm, window_hbm, table_hbm, first_ref, second_ref,
    volt, window, table, filtered, turned, send, recv, unpacked, channel,
    volt_sems, window_sem, table_sems, send_sem, recv_sems, met_sem,
):
    here = Torus()
    me, y = here.flat, here.y
    across = [here.across(dx, dy) for dx in range(2) for dy in range(4) if dx + dy > 0]
    barrier = pltpu.get_barrier_semaphore()

    def volt_copy(run):
        at = 0 if run == 0 else run * 32 + 3
        frames = pl.ds(at, 35 if run == 0 else 32)
        return pltpu.make_async_copy(volt_hbm.at[frames], volt.at[frames], volt_sems.at[run])

    window_copy = pltpu.make_async_copy(window_hbm.at[pl.ds(0, NUM_TAPS)], window, window_sem)
    table_copies = [
        pltpu.make_async_copy(table_hbm.at[lax.rem(y + g, 4)], table.at[g], table_sems.at[g])
        for g in range(4)
    ]
    window_copy.start()
    volt_copy(0).start()
    volt_copy(1).start()

    def greet(dx, dcore, first=0):
        for dz in range(first, 8):
            target = here.away(dx, 0, dz, dcore)[0]
            pl.semaphore_signal(barrier, inc=1, device_id=target, device_id_type=MESH)

    greet(0, 0, 1)
    greet(0, 1)
    greet(2, 0)
    greet(2, 1)
    for target in across:
        pl.semaphore_signal(barrier, inc=1, device_id=target, device_id_type=MESH)
    volt_copy(2).start()
    volt_copy(3).start()
    table_copies[0].start()
    for run in range(4, 8):
        volt_copy(run).start()
    for copy in table_copies[1:]:
        copy.start()

    def filter_run(run):
        volt_copy(run).wait()

        def block(i, carry):
            at = run * 32 + i * 16
            for q in range(4):
                rows = slice(q * 16, (q + 1) * 16)
                taps = [window[t, rows, :] for t in range(NUM_TAPS)]
                frames = []
                for s in range(16 + NUM_TAPS - 1):
                    frames.append(volt[at + s, rows, :].astype(jnp.float32))
                    if s >= NUM_TAPS - 1:
                        terms = [f * tap for f, tap in zip(frames[-NUM_TAPS:], taps)]
                        first = (s - NUM_TAPS + 1) * PITCH
                        total = (terms[0] + terms[1]) + (terms[2] + terms[3])
                        turned[q, first : first + 16, :] = total
                for r in range(16):
                    n, a = q * 4 + r // 4, r % 4
                    to = run // 4 * 512 + a * HALF + run % 4 * 32
                    to = pl.multiple_of(to + i * 16, 16)
                    column = turned[q, pl.ds(r, 16, stride=PITCH), :]
                    filtered[pl.ds(to, 16), n * 128 : (n + 1) * 128] = column.astype(jnp.bfloat16)
            return carry

        lax.fori_loop(0, 2, block, 0)

    def products(g, half):
        parts = []
        for pair in range(2):
            at = half * 512 + pair * 256
            product = lax.dot_general(
                table[g], filtered[at : at + 256, :], (((1,), (1,)), ((), ())),
                preferred_element_type=jnp.float32,
            )
            parts += [product[:, :128].reshape(4, 64, 128), product[:, 128:].reshape(4, 64, 128)]
        return parts

    def transform(g, half):
        block = jnp.concatenate(products(g, half), axis=0)
        send[g, :, half] = jnp.transpose(block, (1, 0, 2)).astype(jnp.bfloat16)

    def transform_channels(g):
        halves = [products(g, 0), products(g, 1)]
        for c in range(2):
            rows = [halves[h][a][c * 2 : c * 2 + 2] for a in range(4) for h in range(2)]
            block = jnp.concatenate(rows, axis=0)
            send[g, :, c] = jnp.transpose(block, (1, 0, 2)).astype(jnp.bfloat16)

    def send_eight(g, tile, dx, dcore, first=0):
        for dz in range(first, 8):
            target, slot = here.away(dx, g, dz, dcore)
            pltpu.make_async_remote_copy(
                src_ref=send.at[g, slot, tile], dst_ref=recv.at[me, tile],
                send_sem=send_sem, recv_sem=recv_sems.at[g, tile],
                device_id=target, device_id_type=MESH,
            ).start()

    def send_group(g, tile, first=0):
        def eight(k, carry):
            send_eight(g, tile, lax.div(k, 2), lax.rem(k, 2))
            return carry

        lax.fori_loop(first, 8, eight, 0)

    def unpack(g, tile):
        got = recv.at[pl.ds(0, 63 if g == 0 else 64), 0]
        pltpu.make_async_copy(got, got, recv_sems.at[g, tile]).wait()
        for z_lo in range(2):
            first = z_lo * 128 + lax.rem(y + 4 - g, 4) * 32
            values = recv[pl.ds(first, 32), tile].astype(jnp.float32) * 0.0625
            unpacked[:512, :] = values.reshape(512, 128)
            to = pl.ds(pl.multiple_of(first * 4, 128), 128)
            for k in range(4):
                part = unpacked[pl.ds(k, 128, stride=4), :].astype(jnp.bfloat16)
                c, half = (k // 2, tile) if g < 2 else (tile, k // 2)
                lanes = k % 2 * 256 + half * 128
                (channel, second_ref)[c][to, lanes : lanes + 128] = part

    window_copy.wait()
    for run in range(4):
        filter_run(run)
    pl.semaphore_wait(barrier, 38)
    for target in across:
        pl.semaphore_signal(met_sem, inc=1, device_id=target, device_id_type=MESH)
    table_copies[0].wait()
    transform(0, 0)
    send_eight(0, 0, 0, 0, 1)
    send_eight(0, 0, 0, 1)
    send_eight(0, 0, 2, 0)
    send_eight(0, 0, 2, 1)
    pl.semaphore_wait(met_sem, 7)
    for dx in (1, 3):
        send_eight(0, 0, dx, 0)
        send_eight(0, 0, dx, 1)
    table_copies[1].wait()
    transform(1, 0)
    send_group(1, 0)
    for run in range(4, 8):
        filter_run(run)
    transform(0, 1)
    send_eight(0, 1, 0, 0, 1)
    send_group(0, 1, 1)
    transform(1, 1)
    send_group(1, 1)
    for g in range(2, 4):
        table_copies[g].wait()
        transform_channels(g)

    def send_one(j, dz):
        tile, g, k = lax.div(j, 16), lax.rem(lax.div(j, 8), 2), lax.rem(j, 8)
        x, core = lax.rem(here.x + lax.div(k, 2), 4), lax.rem(here.core + lax.rem(k, 2), 2)
        inp = here.z_inp[dz] + core
        target = (here.z_chan[dz] + lax.rem(here.y + 2 + g, 4) * 4 + x, inp)
        pltpu.make_async_remote_copy(
            src_ref=send.at[2 + g, here.z_chan[dz] * 2 + x * 8 + inp, tile], dst_ref=recv.at[me, tile],
            send_sem=send_sem, recv_sem=recv_sems.at[2 + g, tile],
            device_id=target, device_id_type=MESH,
        ).start()

    def to_origin(j, dz):
        k = lax.rem(j, 8)
        apart = lax.rem(here.x + lax.div(k, 2), 4) + lax.rem(here.y + 2 + lax.rem(lax.div(j, 8), 2), 4)
        core = lax.rem(here.core + lax.rem(k, 2), 2)
        return apart + here.z_chan[dz] + here.z_inp[dz] + 1 - core == 0

    def rounds(j, carry):
        for dz in range(8):
            lead = jnp.where(to_origin(j, dz), 16, here.lead[dz])

            @pl.when(j < 32 - lead)
            def _():
                send_one(j, dz)

            ahead = 32 - here.lead[dz] + lax.div(j, 4)

            @pl.when((lax.rem(j, 4) == 3) & (ahead < 32))
            def _():
                @pl.when(jnp.logical_not(to_origin(ahead, dz)))
                def _():
                    send_one(ahead, dz)

            @pl.when((j < 16) & to_origin(j, dz))
            def _():
                send_one(j + 16, dz)

        return carry

    lax.fori_loop(0, 32, rounds, 0)
    recv[pl.ds(me, 1)] = send[0, pl.ds(here.slot, 1)]

    for g, tile in ((0, 0), (1, 0), (0, 1), (1, 1), (2, 0), (3, 0)):
        unpack(g, tile)
    for k in range(4):
        gram_rows(channel, first_ref, k)
    unpack(2, 1)
    unpack(3, 1)
    sent = recv.at[pl.ds(0, 255)]
    pltpu.make_async_copy(sent, sent, send_sem).wait()


def spectra_of(voltages, window, table):
    return pl.pallas_call(
        spectra_kernel,
        out_shape=(
            jax.ShapeDtypeStruct((INPUTS, INPUTS), jnp.float32),
            jax.ShapeDtypeStruct((INPUTS, 512), jnp.bfloat16),
        ),
        in_specs=[
            pl.BlockSpec(memory_space=pltpu.HBM),
            pl.BlockSpec(memory_space=pltpu.HBM),
            pl.BlockSpec(memory_space=pltpu.HBM),
        ],
        out_specs=(pl.BlockSpec(memory_space=pltpu.VMEM),) * 2,
        scratch_shapes=[
            pltpu.VMEM((FRAMES, 64, 128), jnp.bfloat16),
            pltpu.VMEM((NUM_TAPS, 64, 128), jnp.float32),
            pltpu.VMEM((4, 256, FFT_LEN), jnp.bfloat16),
            pltpu.VMEM((1024, FFT_LEN), jnp.bfloat16),
            pltpu.VMEM((4, 17 * PITCH + 7, 128), jnp.float32),
            pltpu.VMEM((4, 64, 2, 16, 128), jnp.bfloat16),
            pltpu.VMEM((DEVICES, 2, 16, 128), jnp.bfloat16),
            pltpu.VMEM((520, 128), jnp.float32),
            pltpu.VMEM((INPUTS, 512), jnp.bfloat16),
            pltpu.SemaphoreType.DMA((8,)),
            pltpu.SemaphoreType.DMA,
            pltpu.SemaphoreType.DMA((4,)),
            pltpu.SemaphoreType.DMA,
            pltpu.SemaphoreType.DMA((4, 2)),
            pltpu.SemaphoreType.REGULAR,
        ],
        compiler_params=pltpu.CompilerParams(
            collective_id=0, has_side_effects=True, vmem_limit_bytes=45 << 20
        ),
        name="spectra_exchange",
    )(voltages, window, table)


def gram_kernel(first_ref, in_ref, out_hbm, blocks, first_sems, sems):
    copies = []
    for k in range(2):
        rows = slice(k * 512, (k + 1) * 512)
        copies.append(pltpu.make_async_copy(first_ref.at[rows], out_hbm.at[0, rows], first_sems.at[k]))
        copies[-1].start()
    for k in range(4):
        rows = slice(k * 256, (k + 1) * 256)
        gram_rows(in_ref, blocks, k)
        copies.append(pltpu.make_async_copy(blocks.at[rows], out_hbm.at[1, rows], sems.at[k]))
        copies[-1].start()
    for copy in copies:
        copy.wait()


def gram(first, spectra):
    return pl.pallas_call(
        gram_kernel,
        out_shape=jax.ShapeDtypeStruct((2, INPUTS, INPUTS), jnp.float32),
        in_specs=[pl.BlockSpec(memory_space=pltpu.VMEM)] * 2,
        out_specs=pl.BlockSpec(memory_space=pltpu.HBM),
        scratch_shapes=[
            pltpu.VMEM((INPUTS, INPUTS), jnp.float32),
            pltpu.SemaphoreType.DMA((2,)),
            pltpu.SemaphoreType.DMA((4,)),
        ],
        compiler_params=pltpu.CompilerParams(vmem_limit_bytes=40 << 20),
        name="gram",
    )(first, spectra)


def local(voltages):
    tiles = voltages.reshape(4, FRAMES * 16, 128).transpose(1, 0, 2).reshape(FRAMES, 64, 128)
    return gram(*spectra_of(tiles, jnp.asarray(make_window()), jnp.asarray(make_table())))


def solution(mesh):
    in_specs = (P(("chan", "inp"), None),)
    out_specs = P(("chan", "inp"), None, None)
    return jax.shard_map(local, mesh=mesh, in_specs=in_specs, out_specs=out_specs, check_vma=False)
```

```python
import jax
import jax.numpy as jnp
import numpy as np
from jax import lax
from jax.experimental import pallas as pl
from jax.experimental.pallas import tpu as pltpu
from jax.sharding import PartitionSpec as P

FFT_LEN = 2048
CHANNELS = 512
NUM_TAPS = 4
SPECTRA = 256
FRAMES = SPECTRA + NUM_TAPS - 1
INPUTS = 1024
DEVICES = 256
HALF = SPECTRA // 2
PITCH = 17
WINDOW_PAD = 192
MESH = pl.DeviceIdType.MESH


def make_window():
    index = np.arange(NUM_TAPS * FFT_LEN, dtype=np.float64) + 0.5
    shifted = index / FFT_LEN - NUM_TAPS / 2.0
    taper = 0.54 - 0.46 * np.cos(2.0 * np.pi * index / (NUM_TAPS * FFT_LEN))
    window = (np.sinc(shifted) * taper).astype(np.float32).reshape(NUM_TAPS, 16, 1, 128)
    window = np.broadcast_to(window, (NUM_TAPS, 16, 4, 128)).reshape(NUM_TAPS, 64, 128)
    return np.concatenate([window, np.zeros((WINDOW_PAD - NUM_TAPS, 64, 128), np.float32)])


def make_table():
    bins = np.arange(CHANNELS, dtype=np.int64)[:, None] + FFT_LEN // 8
    phase = (bins * np.arange(FFT_LEN, dtype=np.int64)[None, :] % FFT_LEN) * (2.0 * np.pi / FFT_LEN)
    both = np.stack([np.cos(phase), -np.sin(phase)]) / np.sqrt(FFT_LEN)
    both = both.reshape(2, 2, 4, 32, 2, FFT_LEN).transpose(2, 4, 0, 1, 3, 5)
    return both.reshape(4, 256, FFT_LEN).astype(np.float32).astype(jnp.bfloat16)


class Torus:
    def __init__(self):
        chan, inp = lax.axis_index("chan"), lax.axis_index("inp")
        self.x, self.y = lax.rem(chan, 4), lax.rem(lax.div(chan, 4), 4)
        self.z, self.core = lax.div(inp, 2) * 2 + lax.div(chan, 16), lax.rem(inp, 2)
        self.flat = chan * 8 + inp
        self.slot = lax.div(chan, 16) * 32 + self.x * 8 + inp
        zs = [lax.rem(self.z + dz, 8) for dz in range(8)]
        self.z_chan = [lax.rem(z, 2) * 16 for z in zs]
        self.z_inp = [lax.div(z, 2) * 2 for z in zs]
        self.lead = [jnp.where(z < 2, 6 - z, jnp.where(z == 2, 4, jnp.where(z == 3, 2, 0))) for z in zs]
        self.y_chan = [lax.rem(self.y + dy, 4) * 4 for dy in range(4)]

    def away(self, dx, dy, dz, dcore):
        x, core = lax.rem(self.x + dx, 4), lax.rem(self.core + dcore, 2)
        inp = self.z_inp[dz] + core
        return (self.z_chan[dz] + self.y_chan[dy] + x, inp), self.z_chan[dz] * 2 + x * 8 + inp

    def across(self, dx, dy):
        x = self.x + (1 - 2 * lax.rem(self.x, 2)) * dx
        return self.z_chan[0] + self.y_chan[dy] + x, self.z_inp[0] + self.core


def gram_rows(in_ref, out_ref, k):
    dims = (((1,), (1,)), ((), ()))
    rows = slice(k * 256, (k + 1) * 256)
    real = lax.dot_general(
        in_ref[rows, :], in_ref[k * 256 :, :], dims, preferred_element_type=jnp.float32
    )
    turned = jnp.concatenate([in_ref[rows, 256:], -in_ref[rows, :256]], axis=1)
    imag = lax.dot_general(
        turned, in_ref[: (k + 1) * 256, :], dims, preferred_element_type=jnp.float32
    )
    down = lax.broadcasted_iota(jnp.int32, (256, 256), 0)
    across = lax.broadcasted_iota(jnp.int32, (256, 256), 1)
    if k > 0:
        out_ref[rows, : k * 256] = imag[:, : k * 256]
    out_ref[rows, rows] = jnp.where(down <= across, real[:, :256], imag[:, k * 256 :])
    if k < 3:
        out_ref[rows, (k + 1) * 256 :] = real[:, 256:]


def spectra_kernel(
    volt_hbm, window_hbm, table_hbm, first_ref, second_ref,
    volt, window, table, filtered, turned, send, recv, unpacked, channel,
    volt_sems, window_sem, table_sems, send_sem, recv_sems, met_sem,
):
    here = Torus()
    me, y = here.flat, here.y
    across = [here.across(dx, dy) for dx in range(2) for dy in range(4) if dx + dy > 0]
    barrier = pltpu.get_barrier_semaphore()

    def volt_copy(run):
        at = 0 if run == 0 else run * 32 + 3
        frames = pl.ds(at, 35 if run == 0 else 32)
        return pltpu.make_async_copy(volt_hbm.at[frames], volt.at[frames], volt_sems.at[run])

    window_copy = pltpu.make_async_copy(window_hbm.at[pl.ds(0, NUM_TAPS)], window, window_sem)
    table_copies = [
        pltpu.make_async_copy(table_hbm.at[lax.rem(y + g, 4)], table.at[g], table_sems.at[g])
        for g in range(4)
    ]
    window_copy.start()
    volt_copy(0).start()
    volt_copy(1).start()

    def greet(dx, dcore, first=0):
        for dz in range(first, 8):
            target = here.away(dx, 0, dz, dcore)[0]
            pl.semaphore_signal(barrier, inc=1, device_id=target, device_id_type=MESH)

    greet(0, 0, 1)
    greet(0, 1)
    greet(2, 0)
    greet(2, 1)
    for target in across:
        pl.semaphore_signal(barrier, inc=1, device_id=target, device_id_type=MESH)
    volt_copy(2).start()
    volt_copy(3).start()
    table_copies[0].start()
    for run in range(4, 8):
        volt_copy(run).start()
    for copy in table_copies[1:]:
        copy.start()

    def filter_run(run):
        volt_copy(run).wait()

        def block(i, carry):
            at = run * 32 + i * 16
            for q in range(4):
                rows = slice(q * 16, (q + 1) * 16)
                taps = [window[t, rows, :] for t in range(NUM_TAPS)]
                frames = []
                for s in range(16 + NUM_TAPS - 1):
                    frames.append(volt[at + s, rows, :].astype(jnp.float32))
                    if s >= NUM_TAPS - 1:
                        terms = [f * tap for f, tap in zip(frames[-NUM_TAPS:], taps)]
                        first = (s - NUM_TAPS + 1) * PITCH
                        total = (terms[0] + terms[1]) + (terms[2] + terms[3])
                        turned[q, first : first + 16, :] = total
                for r in range(16):
                    n, a = q * 4 + r // 4, r % 4
                    to = run // 4 * 512 + a * HALF + run % 4 * 32
                    to = pl.multiple_of(to + i * 16, 16)
                    column = turned[q, pl.ds(r, 16, stride=PITCH), :]
                    filtered[pl.ds(to, 16), n * 128 : (n + 1) * 128] = column.astype(jnp.bfloat16)
            return carry

        lax.fori_loop(0, 2, block, 0)

    def products(g, half):
        parts = []
        for pair in range(2):
            at = half * 512 + pair * 256
            product = lax.dot_general(
                table[g], filtered[at : at + 256, :], (((1,), (1,)), ((), ())),
                preferred_element_type=jnp.float32,
            )
            parts += [product[:, :128].reshape(4, 64, 128), product[:, 128:].reshape(4, 64, 128)]
        return parts

    def transform(g, half):
        block = jnp.concatenate(products(g, half), axis=0)
        send[g, :, half] = jnp.transpose(block, (1, 0, 2)).astype(jnp.bfloat16)

    def transform_channels(g):
        halves = [products(g, 0), products(g, 1)]
        for c in range(2):
            rows = [halves[h][a][c * 2 : c * 2 + 2] for a in range(4) for h in range(2)]
            block = jnp.concatenate(rows, axis=0)
            send[g, :, c] = jnp.transpose(block, (1, 0, 2)).astype(jnp.bfloat16)

    def send_eight(g, tile, dx, dcore, first=0):
        for dz in range(first, 8):
            target, slot = here.away(dx, g, dz, dcore)
            pltpu.make_async_remote_copy(
                src_ref=send.at[g, slot, tile], dst_ref=recv.at[me, tile],
                send_sem=send_sem, recv_sem=recv_sems.at[g, tile],
                device_id=target, device_id_type=MESH,
            ).start()

    def send_group(g, tile, first=0):
        def eight(k, carry):
            send_eight(g, tile, lax.div(k, 2), lax.rem(k, 2))
            return carry

        lax.fori_loop(first, 8, eight, 0)

    def unpack(g, tile):
        got = recv.at[pl.ds(0, 63 if g == 0 else 64), 0]
        pltpu.make_async_copy(got, got, recv_sems.at[g, tile]).wait()
        for z_lo in range(2):
            first = z_lo * 128 + lax.rem(y + 4 - g, 4) * 32
            values = recv[pl.ds(first, 32), tile].astype(jnp.float32) * 0.0625
            unpacked[:512, :] = values.reshape(512, 128)
            to = pl.ds(pl.multiple_of(first * 4, 128), 128)
            for k in range(4):
                part = unpacked[pl.ds(k, 128, stride=4), :].astype(jnp.bfloat16)
                c, half = (k // 2, tile) if g < 2 else (tile, k // 2)
                lanes = k % 2 * 256 + half * 128
                (channel, second_ref)[c][to, lanes : lanes + 128] = part

    window_copy.wait()
    for run in range(4):
        filter_run(run)
    pl.semaphore_wait(barrier, 38)
    for target in across:
        pl.semaphore_signal(met_sem, inc=1, device_id=target, device_id_type=MESH)
    table_copies[0].wait()
    transform(0, 0)
    send_eight(0, 0, 0, 0, 1)
    send_eight(0, 0, 0, 1)
    send_eight(0, 0, 2, 0)
    send_eight(0, 0, 2, 1)
    pl.semaphore_wait(met_sem, 7)
    for dx in (1, 3):
        send_eight(0, 0, dx, 0)
        send_eight(0, 0, dx, 1)
    table_copies[1].wait()
    transform(1, 0)
    send_group(1, 0)
    for run in range(4, 8):
        filter_run(run)
    transform(0, 1)
    send_eight(0, 1, 0, 0, 1)
    send_group(0, 1, 1)
    transform(1, 1)
    send_group(1, 1)
    for g in range(2, 4):
        table_copies[g].wait()
        transform_channels(g)

    def send_one(j, dz):
        tile, g, k = lax.div(j, 16), lax.rem(lax.div(j, 8), 2), lax.rem(j, 8)
        x, core = lax.rem(here.x + lax.div(k, 2), 4), lax.rem(here.core + lax.rem(k, 2), 2)
        inp = here.z_inp[dz] + core
        target = (here.z_chan[dz] + lax.rem(here.y + 2 + g, 4) * 4 + x, inp)
        pltpu.make_async_remote_copy(
            src_ref=send.at[2 + g, here.z_chan[dz] * 2 + x * 8 + inp, tile], dst_ref=recv.at[me, tile],
            send_sem=send_sem, recv_sem=recv_sems.at[2 + g, tile],
            device_id=target, device_id_type=MESH,
        ).start()

    def to_origin(j, dz):
        k = lax.rem(j, 8)
        apart = lax.rem(here.x + lax.div(k, 2), 4) + lax.rem(here.y + 2 + lax.rem(lax.div(j, 8), 2), 4)
        core = lax.rem(here.core + lax.rem(k, 2), 2)
        return apart + here.z_chan[dz] + here.z_inp[dz] + 1 - core == 0

    def rounds(j, carry):
        for dz in range(8):
            lead = jnp.where(to_origin(j, dz), 16, here.lead[dz])

            @pl.when(j < 32 - lead)
            def _():
                send_one(j, dz)

            ahead = 32 - here.lead[dz] + lax.div(j, 4)

            @pl.when((lax.rem(j, 4) == 3) & (ahead < 32))
            def _():
                @pl.when(jnp.logical_not(to_origin(ahead, dz)))
                def _():
                    send_one(ahead, dz)

            @pl.when((j < 16) & to_origin(j, dz))
            def _():
                send_one(j + 16, dz)

        return carry

    lax.fori_loop(0, 32, rounds, 0)
    recv[pl.ds(me, 1)] = send[0, pl.ds(here.slot, 1)]

    for g, tile in ((0, 0), (1, 0), (0, 1), (1, 1), (2, 0), (3, 0)):
        unpack(g, tile)
    for k in range(4):
        gram_rows(channel, first_ref, k)
    unpack(2, 1)
    unpack(3, 1)
    sent = recv.at[pl.ds(0, 255)]
    pltpu.make_async_copy(sent, sent, send_sem).wait()


def spectra_of(voltages, window, table):
    return pl.pallas_call(
        spectra_kernel,
        out_shape=(
            jax.ShapeDtypeStruct((INPUTS, INPUTS), jnp.float32),
            jax.ShapeDtypeStruct((INPUTS, 512), jnp.bfloat16),
        ),
        in_specs=[
            pl.BlockSpec(memory_space=pltpu.HBM),
            pl.BlockSpec(memory_space=pltpu.HBM),
            pl.BlockSpec(memory_space=pltpu.HBM),
        ],
        out_specs=(pl.BlockSpec(memory_space=pltpu.VMEM),) * 2,
        scratch_shapes=[
            pltpu.VMEM((FRAMES, 64, 128), jnp.bfloat16),
            pltpu.VMEM((NUM_TAPS, 64, 128), jnp.float32),
            pltpu.VMEM((4, 256, FFT_LEN), jnp.bfloat16),
            pltpu.VMEM((1024, FFT_LEN), jnp.bfloat16),
            pltpu.VMEM((4, 17 * PITCH + 7, 128), jnp.float32),
            pltpu.VMEM((4, 64, 2, 16, 128), jnp.bfloat16),
            pltpu.VMEM((DEVICES, 2, 16, 128), jnp.bfloat16),
            pltpu.VMEM((520, 128), jnp.float32),
            pltpu.VMEM((INPUTS, 512), jnp.bfloat16),
            pltpu.SemaphoreType.DMA((8,)),
            pltpu.SemaphoreType.DMA,
            pltpu.SemaphoreType.DMA((4,)),
            pltpu.SemaphoreType.DMA,
            pltpu.SemaphoreType.DMA((4, 2)),
            pltpu.SemaphoreType.REGULAR,
        ],
        compiler_params=pltpu.CompilerParams(
            collective_id=0, has_side_effects=True, vmem_limit_bytes=45 << 20
        ),
        name="spectra_exchange",
    )(voltages, window, table)


def gram_kernel(first_ref, in_ref, out_hbm, blocks, first_sems, sems):
    copies = []
    for k in range(2):
        rows = slice(k * 512, (k + 1) * 512)
        copies.append(pltpu.make_async_copy(first_ref.at[rows], out_hbm.at[0, rows], first_sems.at[k]))
        copies[-1].start()
    for k in range(4):
        rows = slice(k * 256, (k + 1) * 256)
        gram_rows(in_ref, blocks, k)
        copies.append(pltpu.make_async_copy(blocks.at[rows], out_hbm.at[1, rows], sems.at[k]))
        copies[-1].start()
    for copy in copies:
        copy.wait()


def gram(first, spectra):
    return pl.pallas_call(
        gram_kernel,
        out_shape=jax.ShapeDtypeStruct((2, INPUTS, INPUTS), jnp.float32),
        in_specs=[pl.BlockSpec(memory_space=pltpu.VMEM)] * 2,
        out_specs=pl.BlockSpec(memory_space=pltpu.HBM),
        scratch_shapes=[
            pltpu.VMEM((INPUTS, INPUTS), jnp.float32),
            pltpu.SemaphoreType.DMA((2,)),
            pltpu.SemaphoreType.DMA((4,)),
        ],
        compiler_params=pltpu.CompilerParams(vmem_limit_bytes=40 << 20),
        name="gram",
    )(first, spectra)


def local(voltages):
    tiles = voltages.reshape(4, FRAMES * 16, 128).transpose(1, 0, 2).reshape(FRAMES, 64, 128)
    return gram(*spectra_of(tiles, jnp.asarray(make_window()), jnp.asarray(make_table())))


def solution(mesh):
    in_specs = (P(("chan", "inp"), None),)
    out_specs = P(("chan", "inp"), None, None)
    return jax.shard_map(local, mesh=mesh, in_specs=in_specs, out_specs=out_specs, check_vma=False)
```
